32 devices in a mesh: groups: 2 (over y), ctx: 4 (over z), head: 2 (over x), row: 2 (over core).
Axes of the slice: x: 2, y: 2, z: 4, core: 2. Of those that a mesh axis runs over, the one named last changes fastest.
Arguments:
- residual: bfloat16 [512, 5120], P(('groups', 'ctx', 'row')), parts along dimension 0, may hold values from -6 to 6
- queries: bfloat16 [512, 20, 128], P('groups', 'head'), parts along dimension 0, may hold values from -160 to 160
- incoming_keys: bfloat16 [512, 4, 128], P(('groups', 'ctx', 'row'), 'head'), parts along dimension 0, may hold values from -6 to 6
- incoming_values: bfloat16 [512, 4, 128], P(('groups', 'ctx', 'row'), 'head'), parts along dimension 0, may hold values from -6 to 6
- cache_keys: bfloat16 [32768, 4, 128], P(('groups', 'ctx', 'row'), 'head'), parts along dimension 0, may hold values from -7 to 7
- cached_value_rows: bfloat16 [32768, 4, 128], P(('groups', 'ctx', 'row'), 'head'), parts along dimension 0, may hold values from -6 to 6
- context: int32 [2], P('groups'), parts along dimension 0, may hold values from 4096 to 16384
- attention_out: bfloat16 [2560, 5120], P('head', ('ctx', 'row')), may hold values from -1.5 to 1.5
- mixer_input: bfloat16 [512, 32, 128], P('groups', 'head', ('ctx', 'row')), parts along dimension 0, may hold values from -6 to 6
- mixer_gate: bfloat16 [512, 32, 128], P('groups', 'head', ('ctx', 'row')), parts along dimension 0, may hold values from -6 to 6
- state_in: bfloat16 [512, 256], P('groups'), parts along dimension 0, may hold values from -6 to 6
- state_out: bfloat16 [512, 256], P('groups'), parts along dimension 0, may hold values from -1.5 to 1.5
- step_size: float32 [512, 32], P('groups', 'head'), parts along dimension 0, may hold values from 0 to 2, as said below
- decay_log: float32 [32], P('head'), may hold values from -1 to 1
- skip_gain: float32 [32], P('head'), may hold values from 0.5 to 1.5
- prior_state: float32 [64, 128, 256], P(('groups', 'head'), ('ctx', 'row')), parts along dimension 0, may hold values from -1.5 to 1.5
- mixer_out: bfloat16 [4096, 5120], P('head', ('ctx', 'row')), may hold values from -0.09375 to 0.09375
- norm_gain: float32 [5120], replicated, may hold values from 0.5 to 1.5
- hidden_gate: bfloat16 [5120, 21504], P('head', ('ctx', 'row')), may hold values from -0.078125 to 0.078125
- hidden_up: bfloat16 [5120, 21504], P('head', ('ctx', 'row')), may hold values from -0.078125 to 0.078125
- hidden_down: bfloat16 [21504, 5120], P(('ctx', 'row'), 'head'), may hold values from -0.0390625 to 0.0390625
Outputs:
- block_out: bfloat16 [512, 5120], P(('groups', 'ctx', 'row'), 'head'), parts along dimension 0
The draws below stay inside these ranges and needn't reach their ends.
There are 2 independent parts, one for each index of `groups`. The reference program is written for one: setup_inputs(seed, part) draws one part's arguments, and reference() takes and returns one part's arrays. A program takes and returns all parts, laid end to end along the dimension named above; an argument that names none is the same for every part. Nothing has to cross between parts.
Inputs may be any that keep to these rules, and one draw needn't show every extreme that they name: The cached slots below context are valid; the new tokens follow them. `step_size`: positive.
All inputs are finite; a program needn't handle non-finite values.
Results may differ from the reference program's by a relative error of at most 0.01.
Values may be sent and summed in bfloat16 or wider, within the bound.
A program may use at most 128 MiB of HBM per device.

```python
import math
import jax
import jax.numpy as jnp
from jax import lax

D = 5120
QUERY_HEADS = 20
KEY_VALUE_HEADS = 4
HEAD_SIZE = 128
STATE_HEADS = 32
SP = 128
NS = 256
FF = 21504
NEW_TOKENS = 256
CTX_DEV = 2048
CACHED_SLOTS = 16384


def shared_keys(key):
    starting_keys = jax.random.truncated_normal(jax.random.fold_in(key, 101), -6.0, 6.0, (CACHED_SLOTS, KEY_VALUE_HEADS, HEAD_SIZE), jnp.float32)
    return starting_keys


def draw_cache_keys(key, part):
    return shared_keys(key).astype(jnp.bfloat16)


def draw_queries(key, part):
    query_rows = 2.5 * jax.random.truncated_normal(jax.random.fold_in(key, 104), -6.0, 6.0, (NEW_TOKENS, QUERY_HEADS, HEAD_SIZE), jnp.float32)
    return query_rows.astype(jnp.bfloat16)


def draw_step_size(key, part):
    lower_end = -6.9
    upper_end = -2.3
    head_fraction = jnp.exp(jax.random.uniform(jax.random.fold_in(key, 111), (1, STATE_HEADS), jnp.float32, lower_end, upper_end))
    coarse_multiplier = jnp.exp(jax.random.uniform(jax.random.fold_in(key, 112), (NEW_TOKENS, STATE_HEADS), jnp.float32, -0.7, 0.7))
    spike_rows = jax.random.randint(jax.random.fold_in(key, 113), (3,), 0, NEW_TOKENS)
    spike_addition = jnp.zeros((NEW_TOKENS, STATE_HEADS), jnp.float32).at[spike_rows].add(0.5)
    return head_fraction * coarse_multiplier + spike_addition


def levels(key, extent, split, least, top_value):
    factor_of = 1.0
    for axis_at, shards_of in split:
        steps = jax.random.uniform(jax.random.fold_in(jax.random.fold_in(key, 6), axis_at), (shards_of,), jnp.float32, least / len(split), top_value / len(split))
        factor_of = factor_of * jnp.repeat(jnp.exp(steps), extent[axis_at] // shards_of).reshape((-1,) + (1,) * (len(extent) - 1 - axis_at))
    return factor_of


def noise(rng, dims, width, reach, shards=(), held_as=jnp.bfloat16):
    drawn = jax.random.normal(rng, dims, jnp.float32) * width
    if len(shards) > 0:
        drawn = levels(rng, dims, shards, -0.22, 0.18) * drawn
    return jnp.clip(drawn, min=-reach, max=reach).astype(held_as)


def setup_inputs(seed: int = 0, part: int = 0) -> dict:
    seeds = jax.random.split(jax.random.key(seed), 22)
    part_keys = jax.random.split(jax.random.fold_in(seeds[21], part), 22)
    return {
        "residual": noise(part_keys[0], (NEW_TOKENS, D), 1.0, 6.0, ((0, 8),)),
        "queries": draw_queries(jax.random.fold_in(jax.random.fold_in(seeds[21], part), 71), part),
        "incoming_keys": noise(part_keys[2], (NEW_TOKENS, KEY_VALUE_HEADS, HEAD_SIZE), 1.0, 6.0, ((0, 8), (1, 2))),
        "incoming_values": noise(part_keys[3], (NEW_TOKENS, KEY_VALUE_HEADS, HEAD_SIZE), 1.0, 6.0, ((0, 8), (1, 2))),
        "cache_keys": draw_cache_keys(jax.random.fold_in(jax.random.fold_in(seeds[21], part), 71), part),
        "cached_value_rows": noise(part_keys[5], (CACHED_SLOTS, KEY_VALUE_HEADS, HEAD_SIZE), 1.0, 6.0, ((0, 8), (1, 2))),
        "context": jax.random.randint(part_keys[6], (1,), CACHED_SLOTS // 4, CACHED_SLOTS + 1).astype(jnp.int32),
        "attention_out": noise(seeds[7], (QUERY_HEADS * HEAD_SIZE, D), 0.25, 1.5, ((0, 2), (1, 8))),
        "mixer_input": noise(part_keys[8], (NEW_TOKENS, STATE_HEADS, SP), 1.0, 6.0, ((1, 2), (2, 8))),
        "mixer_gate": noise(part_keys[9], (NEW_TOKENS, STATE_HEADS, SP), 1.0, 6.0, ((1, 2), (2, 8))),
        "state_in": noise(part_keys[10], (NEW_TOKENS, NS), 1.0, 6.0),
        "state_out": noise(part_keys[11], (NEW_TOKENS, NS), 0.25, 1.5),
        "step_size": draw_step_size(jax.random.fold_in(jax.random.fold_in(seeds[21], part), 71), part),
        "decay_log": jnp.clip(jax.random.uniform(seeds[13], (STATE_HEADS,), jnp.float32, -1.0, 1.0) * levels(seeds[13], (STATE_HEADS,), ((0, 2),), -0.4, 0.0), -1.0, 1.0),
        "skip_gain": jnp.clip(0.5 + 1.0 * jax.random.uniform(seeds[14], (STATE_HEADS,), jnp.float32) ** levels(seeds[14], (STATE_HEADS,), ((0, 2),), -0.2, 0.2), 0.5, 1.5),
        "prior_state": noise(part_keys[15], (STATE_HEADS, SP, NS), 0.25, 1.5, ((0, 2), (1, 8)), jnp.float32),
        "mixer_out": noise(seeds[16], (STATE_HEADS * SP, D), (STATE_HEADS * SP) ** -0.5, 0.09375, ((0, 2), (1, 8))),
        "norm_gain": jnp.clip(1.0 + 0.1 * jax.random.normal(seeds[17], (D,), jnp.float32), 0.5, 1.5),
        "hidden_gate": noise(seeds[18], (D, FF), D ** -0.5, 0.078125, ((0, 2), (1, 8))),
        "hidden_up": noise(seeds[19], (D, FF), D ** -0.5, 0.078125, ((0, 2), (1, 8))),
        "hidden_down": noise(seeds[20], (FF, D), FF ** -0.5, 0.0390625, ((0, 8), (1, 2))),
    }


very_low = -1e+30

def absorb(partial_state, scores, visible, block_values):
    running_sum, weight_total, running_peak = partial_state
    masked = jnp.where(visible, scores, very_low)
    top_score = jnp.maximum(running_peak, lax.optimization_barrier(jnp.max(masked, axis=-1)))
    weights = jnp.where(visible, jnp.exp(masked - top_score[..., None]), 0.0)
    fade_factor = jnp.exp(running_peak - top_score)
    rounded = lax.optimization_barrier(weights.astype(jnp.bfloat16))
    mixed_values = jnp.einsum('tgk,kd->tgd', rounded.astype(jnp.float32), block_values.astype(jnp.float32))
    return (running_sum * fade_factor[..., None] + mixed_values, weight_total * fade_factor + lax.optimization_barrier(jnp.sum(weights, axis=-1)), top_score)

def attend_group(query_rows, keys_all, values_all, fresh_keys, fresh_values, context):
    score_scale = 1.0 / math.sqrt(HEAD_SIZE)
    group_width = query_rows.shape[1]
    query_wide = query_rows.astype(jnp.float32)
    blocks = CACHED_SLOTS // CTX_DEV
    key_blocks = keys_all.reshape(blocks, CTX_DEV, HEAD_SIZE)
    value_blocks = values_all.reshape(blocks, CTX_DEV, HEAD_SIZE)

    def visit_block(partial_state, inputs):
        block_keys, block_values, block_number = inputs
        scores = jnp.einsum('tgd,kd->tgk', query_wide, block_keys.astype(jnp.float32)) * score_scale
        position = block_number * CTX_DEV + jnp.arange(CTX_DEV)
        visible = (position < context[0])[None, None, :]
        return (absorb(partial_state, scores, visible, block_values), None)
    start_state = (jnp.zeros((NEW_TOKENS, group_width, HEAD_SIZE), jnp.float32), jnp.zeros((NEW_TOKENS, group_width), jnp.float32), jnp.full((NEW_TOKENS, group_width), very_low, jnp.float32))
    partial_state = lax.scan(visit_block, start_state, (key_blocks, value_blocks, jnp.arange(blocks)))[0]
    fresh_scores = jnp.einsum('tgd,kd->tgk', query_wide, fresh_keys.astype(jnp.float32)) * score_scale
    token_order = jnp.arange(NEW_TOKENS)
    fresh_visible = (token_order[None, :] <= token_order[:, None])[:, None, :]
    running_sum, weight_total, running_peak = absorb(partial_state, fresh_scores, fresh_visible, fresh_values)
    return (running_sum / weight_total[..., None]).astype(jnp.bfloat16)

def scan_mixer(mixer_input, mixer_gate, state_in, state_out, step_size, decay_log, skip_gain, prior_state):
    tokens = mixer_input.shape[0]
    decay_rate = -jnp.exp(decay_log)
    log_fade = jnp.cumsum(step_size * decay_rate[None, :], axis=0)
    token_order = jnp.arange(tokens)
    causal_mask = token_order[:, None] >= token_order[None, :]
    fade_heads = jnp.transpose(log_fade)
    differ = fade_heads[:, :, None] - fade_heads[:, None, :]
    lower_fade = jnp.exp(jnp.where(causal_mask[None], differ, very_low))
    state_match = jnp.einsum('tn,sn->ts', state_out.astype(jnp.float32), state_in.astype(jnp.float32))
    mixing = lower_fade * state_match[None]
    inputs_wide = mixer_input.astype(jnp.float32)
    scaled = step_size[:, :, None] * inputs_wide
    inner_part = jnp.einsum('hts,shp->thp', mixing, scaled, precision=lax.Precision.HIGHEST)
    carried = jnp.einsum('tn,hpn->thp', state_out.astype(jnp.float32), prior_state, precision=lax.Precision.HIGHEST) * jnp.exp(log_fade)[:, :, None]
    mixed_out = inner_part + carried + skip_gain[None, :, None] * inputs_wide
    return (mixed_out * jax.nn.silu(mixer_gate.astype(jnp.float32))).astype(jnp.bfloat16)

def reference(residual, queries, incoming_keys, incoming_values, cache_keys, cached_value_rows, context, attention_out, mixer_input, mixer_gate, state_in, state_out, step_size, decay_log, skip_gain, prior_state, mixer_out, norm_gain, hidden_gate, hidden_up, hidden_down):
    group_width = QUERY_HEADS // KEY_VALUE_HEADS
    query_head_count = jnp.transpose(queries.reshape(NEW_TOKENS, KEY_VALUE_HEADS, group_width, HEAD_SIZE), (1, 0, 2, 3))
    key_heads = jnp.transpose(cache_keys, (1, 0, 2))
    value_heads = jnp.transpose(cached_value_rows, (1, 0, 2))
    fresh_keys = jnp.transpose(incoming_keys, (1, 0, 2))
    fresh_values = jnp.transpose(incoming_values, (1, 0, 2))

    def one_head(inputs):
        return attend_group(inputs[0], inputs[1], inputs[2], inputs[3], inputs[4], context)
    attended = lax.map(one_head, (query_head_count, key_heads, value_heads, fresh_keys, fresh_values))
    attended_flat = jnp.transpose(attended, (1, 0, 2, 3)).reshape(NEW_TOKENS, QUERY_HEADS * HEAD_SIZE)
    attention_part = jnp.dot(attended_flat, attention_out, preferred_element_type=jnp.float32)
    gated = scan_mixer(mixer_input, mixer_gate, state_in, state_out, step_size, decay_log, skip_gain, prior_state)
    mixer_part = jnp.dot(gated.reshape(NEW_TOKENS, STATE_HEADS * SP), mixer_out, preferred_element_type=jnp.float32)
    trunk = (residual.astype(jnp.float32) + attention_part + mixer_part).astype(jnp.bfloat16)
    trunk_wide = trunk.astype(jnp.float32)
    inverse_rms = lax.rsqrt(lax.optimization_barrier(jnp.mean(trunk_wide * trunk_wide, axis=1, keepdims=True)) + 1e-05)
    normed = (trunk_wide * inverse_rms * norm_gain[None, :]).astype(jnp.bfloat16)
    gate_sums = jnp.dot(normed, hidden_gate, preferred_element_type=jnp.float32)
    up_sums = jnp.dot(normed, hidden_up, preferred_element_type=jnp.float32)
    hidden = (jax.nn.silu(gate_sums) * up_sums).astype(jnp.bfloat16)
    down_sums = jnp.dot(hidden, hidden_down, preferred_element_type=jnp.float32)
    return (trunk_wide + down_sums).astype(jnp.bfloat16)
```

```python
import math

import jax
import jax.numpy as jnp
from jax import lax
from jax.sharding import PartitionSpec as P

very_low = -1e30


def combined_all(part, axis, combine):
    gathered = jax.tree.map(lambda a: lax.all_gather(a, axis), part)

    def take(source):
        return jax.tree.map(lambda a: lax.dynamic_index_in_dim(a, source, 0, False), gathered)

    return lax.fori_loop(
        1, lax.axis_size(axis), lambda source, state: combine(state, take(source)), take(0)
    )


def absorb(partial_state, scores, visible, block_values):
    running_sum, weight_total, running_peak = partial_state
    masked = jnp.where(visible, scores, very_low)
    top_score = jnp.maximum(running_peak, jnp.max(masked, axis=3))
    weights = jnp.where(visible, jnp.exp(masked - top_score[..., None]), 0.0)
    fade_factor = jnp.exp(running_peak - top_score)
    mixed_values = jnp.einsum(
        "kgts,skd->kgtd",
        weights.astype(jnp.bfloat16),
        block_values,
        preferred_element_type=jnp.float32,
    )
    return (
        running_sum * fade_factor[..., None] + mixed_values,
        weight_total * fade_factor + jnp.sum(weights, axis=3),
        top_score,
    )


def join_partial(first, second):
    sum_first, total_first, peak_first = first
    sum_second, total_second, peak_second = second
    common = jnp.maximum(peak_first, peak_second)
    fade_first = jnp.exp(peak_first - common)
    fade_second = jnp.exp(peak_second - common)
    return (
        sum_first * fade_first[..., None] + sum_second * fade_second[..., None],
        total_first * fade_first + total_second * fade_second,
        common,
    )


def scan_mixer(
    mixer_input, mixer_gate, state_in, state_out, step_size, decay_log, skip_gain, prior_state
):
    tokens = mixer_input.shape[0]
    decay_rate = -jnp.exp(decay_log)
    token_order = jnp.arange(tokens)
    causal_mask = token_order[:, None] >= token_order[None, :]
    log_fade = jnp.dot(
        causal_mask.astype(jnp.float32),
        step_size * decay_rate[None, :],
        precision=lax.Precision.HIGHEST,
    )
    fade_heads = jnp.transpose(log_fade)
    differ = fade_heads[:, :, None] - fade_heads[:, None, :]
    lower_fade = jnp.exp(jnp.where(causal_mask[None], differ, very_low))
    state_match = jnp.einsum("tn,sn->ts", state_out, state_in, preferred_element_type=jnp.float32)
    mixing = lower_fade * state_match[None]
    inputs_wide = mixer_input.astype(jnp.float32)
    scaled = step_size[:, :, None] * inputs_wide
    inner_part = jnp.einsum("hts,shp->thp", mixing, scaled, precision=lax.Precision.HIGHEST)
    carried = (
        jnp.einsum(
            "tn,hpn->thp",
            state_out.astype(jnp.float32),
            prior_state,
            precision=lax.Precision.HIGHEST,
        )
        * jnp.exp(log_fade)[:, :, None]
    )
    mixed_out = inner_part + carried + skip_gain[None, :, None] * inputs_wide
    return (mixed_out * jax.nn.silu(mixer_gate.astype(jnp.float32))).astype(jnp.bfloat16)


def on_device(
    residual,
    queries,
    incoming_keys,
    incoming_values,
    cache_keys,
    cached_value_rows,
    context,
    attention_out,
    mixer_input,
    mixer_gate,
    state_in,
    state_out,
    step_size,
    decay_log,
    skip_gain,
    prior_state,
    mixer_out,
    norm_gain,
    hidden_gate,
    hidden_up,
    hidden_down,
):
    tokens = queries.shape[0]
    head_depth = queries.shape[2]
    shared_heads = cache_keys.shape[1]
    group_width = queries.shape[1] // shared_heads
    local_span = cache_keys.shape[0]
    fresh_count = incoming_keys.shape[0]
    owner_index = lax.axis_index(("ctx", "row"))
    score_scale = 1.0 / math.sqrt(head_depth)
    query_view = queries.reshape(tokens, shared_heads, group_width, head_depth)
    block_size = min(512, local_span)
    blocks = local_span // block_size
    key_blocks = cache_keys.reshape(blocks, block_size, shared_heads, head_depth)
    value_blocks = cached_value_rows.reshape(blocks, block_size, shared_heads, head_depth)

    def visit_block(partial_state, inputs):
        block_keys, block_values, block_number = inputs
        scores = (
            jnp.einsum("tkgd,skd->kgts", query_view, block_keys, preferred_element_type=jnp.float32)
            * score_scale
        )
        position = owner_index * local_span + block_number * block_size + jnp.arange(block_size)
        visible = (position < context[0])[None, None, None, :]
        return (absorb(partial_state, scores, visible, block_values), None)

    start_state = (
        jnp.zeros((shared_heads, group_width, tokens, head_depth), jnp.float32),
        jnp.zeros((shared_heads, group_width, tokens), jnp.float32),
        jnp.full((shared_heads, group_width, tokens), very_low, jnp.float32),
    )
    partial_state = lax.scan(
        visit_block, start_state, (key_blocks, value_blocks, jnp.arange(blocks))
    )[0]
    fresh_scores = (
        jnp.einsum("tkgd,skd->kgts", query_view, incoming_keys, preferred_element_type=jnp.float32)
        * score_scale
    )
    source = owner_index * fresh_count + jnp.arange(fresh_count)
    fresh_visible = (source[None, :] <= jnp.arange(tokens)[:, None])[None, None]
    running_sum, weight_total, running_peak = absorb(
        partial_state, fresh_scores, fresh_visible, incoming_values
    )
    merged = combined_all((running_sum, weight_total, running_peak), ("ctx", "row"), join_partial)
    attended = (merged[0] / merged[1][..., None]).astype(jnp.bfloat16)
    attention_part = jnp.einsum(
        "kgtd,kgdc->tc",
        attended,
        attention_out.reshape(shared_heads, group_width, head_depth, -1),
        preferred_element_type=jnp.float32,
    )
    gated = scan_mixer(
        mixer_input, mixer_gate, state_in, state_out, step_size, decay_log, skip_gain, prior_state
    )
    mixer_rows = mixer_out.reshape(mixer_input.shape[1], -1, mixer_out.shape[1])
    mixer_part = jnp.einsum(
        "thp,hpc->tc",
        lax.all_gather(gated, ("ctx", "row"), axis=2, tiled=True),
        mixer_rows,
        preferred_element_type=jnp.float32,
    )
    branches = attention_part + mixer_part
    summed = lax.psum(branches, "head")
    combined = lax.all_to_all(summed, ("ctx", "row"), split_axis=0, concat_axis=1, tiled=True)
    trunk = (residual.astype(jnp.float32) + combined).astype(jnp.bfloat16)
    trunk_wide = trunk.astype(jnp.float32)
    inverse_rms = lax.rsqrt(jnp.mean(trunk_wide * trunk_wide, axis=1, keepdims=True) + 1e-05)
    normed = (trunk_wide * inverse_rms * norm_gain[None, :]).astype(jnp.bfloat16)
    column_count = hidden_gate.shape[0]
    column_start = lax.axis_index("head") * column_count
    normed_part = lax.dynamic_slice_in_dim(normed, column_start, column_count, 1)
    segment = lax.all_gather(normed_part, ("ctx", "row"), axis=0, tiled=True)
    pair_partial = jnp.stack(
        [
            jnp.dot(segment, hidden_gate, preferred_element_type=jnp.float32),
            jnp.dot(segment, hidden_up, preferred_element_type=jnp.float32),
        ]
    )
    pair_share = lax.psum_scatter(pair_partial, "head", scatter_dimension=1, tiled=True)
    hidden_share = (jax.nn.silu(pair_share[0]) * pair_share[1]).astype(jnp.bfloat16)
    hidden = lax.all_gather(hidden_share, "head", axis=0, tiled=True)
    down_rows = lax.psum_scatter(
        jnp.dot(hidden, hidden_down, preferred_element_type=jnp.float32),
        ("ctx", "row"),
        scatter_dimension=0,
        tiled=True,
    )
    trunk_part = lax.dynamic_slice_in_dim(trunk_wide, column_start, column_count, 1)
    return (trunk_part + down_rows).astype(jnp.bfloat16)


def solution(mesh):
    in_specs = (
        P(("groups", "ctx", "row"), None),
        P("groups", "head", None),
        P(("groups", "ctx", "row"), "head", None),
        P(("groups", "ctx", "row"), "head", None),
        P(("groups", "ctx", "row"), "head", None),
        P(("groups", "ctx", "row"), "head", None),
        P("groups"),
        P("head", ("ctx", "row")),
        P("groups", "head", ("ctx", "row")),
        P("groups", "head", ("ctx", "row")),
        P("groups", None),
        P("groups", None),
        P("groups", "head"),
        P("head"),
        P("head"),
        P(("groups", "head"), ("ctx", "row"), None),
        P("head", ("ctx", "row")),
        P(),
        P("head", ("ctx", "row")),
        P("head", ("ctx", "row")),
        P(("ctx", "row"), "head"),
    )
    out_specs = P(("groups", "ctx", "row"), "head")
    return jax.shard_map(
        on_device, mesh=mesh, in_specs=in_specs, out_specs=out_specs, check_vma=False
    )
```

```python
import functools
import math

import jax
import jax.numpy as jnp
from jax import lax
from jax.experimental import pallas as pl
from jax.experimental.pallas import tpu as pltpu
from jax.sharding import PartitionSpec as P

very_low = -1e30
least_peak = -1e29
owners = ("ctx", "row")
lanes = 128
vmem_limit = 48 * 1024 * 1024


def params():
    return pltpu.CompilerParams(vmem_limit_bytes=vmem_limit)


def in_thirds(x):
    first = x.astype(jnp.bfloat16)
    rest = x - first.astype(jnp.float32)
    second = rest.astype(jnp.bfloat16)
    third = (rest - second.astype(jnp.float32)).astype(jnp.bfloat16)
    return [t.astype(jnp.float32) for t in (first, second, third)]


def attend_kernel(
    heads, scale, place_ref, q_ref, k_ref, v_ref, fk_ref, fv_ref, out_ref, stats_ref
):
    head = pl.program_id(0)
    tokens, depth = q_ref.shape
    span, fresh = k_ref.shape[0], fk_ref.shape[0]
    across = (((1,), (1,)), ((), ()))
    query = q_ref[...]
    valid = place_ref[0]
    first_fresh = place_ref[1]
    scores = lax.dot_general(query, k_ref[...], across, preferred_element_type=jnp.float32) * scale
    position = lax.broadcasted_iota(jnp.int32, (1, span), 1)
    scores = jnp.where(position < valid, scores, very_low)
    new_scores = (
        lax.dot_general(query, fk_ref[...], across, preferred_element_type=jnp.float32) * scale
    )
    source = lax.broadcasted_iota(jnp.int32, (tokens, fresh), 1) + first_fresh
    target = lax.broadcasted_iota(jnp.int32, (tokens, fresh), 0)
    new_scores = jnp.where(source <= target, new_scores, very_low)
    peak = jnp.maximum(
        jnp.max(scores, axis=1, keepdims=True), jnp.max(new_scores, axis=1, keepdims=True)
    )
    peak = jnp.maximum(peak, least_peak)
    weights = jnp.exp(scores - peak)
    new_weights = jnp.exp(new_scores - peak)
    total = jnp.sum(weights, axis=1, keepdims=True) + jnp.sum(new_weights, axis=1, keepdims=True)
    mixed = jnp.dot(
        weights.astype(jnp.bfloat16), v_ref[...], preferred_element_type=jnp.float32
    ) + jnp.dot(new_weights.astype(jnp.bfloat16), fv_ref[...], preferred_element_type=jnp.float32)
    out_ref[:, pl.ds(pl.multiple_of(head * depth, depth), depth)] = (
        mixed / jnp.maximum(total, 1.0)
    ).astype(jnp.bfloat16)

    @pl.when(head == 0)
    def _():
        stats_ref[...] = jnp.zeros_like(stats_ref)

    lane = lax.broadcasted_iota(jnp.int32, stats_ref.shape, 1)
    held = stats_ref[...]
    for i, term in enumerate(in_thirds(peak) + in_thirds(total)):
        held = jnp.where(lane == head + i * heads, term, held)
    stats_ref[...] = held

    @pl.when(head == heads - 1)
    def _():
        out_ref[:, heads * depth :] = held.astype(jnp.bfloat16)


def attend(query_rows, keys, values, fresh_keys, fresh_values, place, heads, shared_heads):
    tokens = query_rows.shape[0]
    depth = query_rows.shape[1] // heads
    width = heads // shared_heads
    stat_lanes = -(-6 * heads // lanes) * lanes
    span, fresh = keys.shape[0], fresh_keys.shape[0]

    def of_group(rows):
        return pl.BlockSpec((rows, depth), lambda j: (0, j // width))

    out = (tokens, heads * depth + stat_lanes)
    return pl.pallas_call(
        functools.partial(attend_kernel, heads, 1.0 / math.sqrt(depth)),
        grid=(heads,),
        in_specs=[
            pl.BlockSpec(memory_space=pltpu.SMEM),
            pl.BlockSpec((tokens, depth), lambda j: (0, j)),
            of_group(span),
            of_group(span),
            of_group(fresh),
            of_group(fresh),
        ],
        out_specs=pl.BlockSpec(out, lambda j: (0, 0)),
        out_shape=jax.ShapeDtypeStruct(out, jnp.bfloat16),
        scratch_shapes=[pltpu.VMEM((tokens, stat_lanes), jnp.float32)],
        compiler_params=params(),
        name="attend",
        cost_estimate=pl.CostEstimate(
            flops=4 * tokens * heads * depth * span,
            bytes_accessed=4 * span * shared_heads * depth + 4 * tokens * heads * depth,
            transcendentals=tokens * heads * span,
        ),
    )(place, query_rows, keys, values, fresh_keys, fresh_values)


def join_kernel(heads, depth, in_ref, out_ref):
    stats = in_ref[:, :, heads * depth :].astype(jnp.float32)
    for j in range(heads):
        peak, total = (
            sum(stats[:, :, k * heads + j : k * heads + j + 1] for k in range(i, i + 3))
            for i in (0, 3)
        )
        share = total * jnp.exp(peak - jnp.max(peak, axis=0, keepdims=True))
        share = share / jnp.sum(share, axis=0, keepdims=True)
        piece = in_ref[:, :, j * depth : (j + 1) * depth].astype(jnp.float32)
        out_ref[:, j * depth : (j + 1) * depth] = jnp.sum(piece * share, axis=0).astype(
            jnp.bfloat16
        )


def join(parts, heads, depth):
    return pl.pallas_call(
        functools.partial(join_kernel, heads, depth),
        out_shape=jax.ShapeDtypeStruct((parts.shape[1], heads * depth), jnp.bfloat16),
        compiler_params=params(),
        name="join",
    )(parts)


def mixer_kernel(
    channels, x_ref, gate_ref, in_ref, read_ref, step_ref, turned_ref, decay_ref, decay_turned_ref,
    skip_ref, prior_ref, out_ref,
):
    tokens, columns = x_ref.shape
    heads = step_ref.shape[1]
    across = (((1,), (1,)), ((), ()))
    row = lax.broadcasted_iota(jnp.int32, (tokens, tokens), 0)
    col = lax.broadcasted_iota(jnp.int32, (tokens, tokens), 1)
    causal = row >= col
    exact = functools.partial(
        jnp.dot, precision=lax.Precision.HIGHEST, preferred_element_type=jnp.float32
    )
    step = step_ref[...]
    fade = exact(causal.astype(jnp.float32), step * -jnp.exp(decay_ref[...]))
    fade_turned = exact(
        turned_ref[...] * -jnp.exp(decay_turned_ref[...]), (row <= col).astype(jnp.float32)
    )
    owner = lax.broadcasted_iota(jnp.int32, (heads, columns), 0) * channels
    column = lax.broadcasted_iota(jnp.int32, (heads, columns), 1)
    spread = ((column >= owner) & (column < owner + channels)).astype(jnp.float32)
    x = x_ref[...].astype(jnp.float32)
    scaled = exact(step, spread) * x
    match = lax.dot_general(
        read_ref[...], in_ref[...], across, preferred_element_type=jnp.float32
    )
    total = skip_ref[...] * x + exact(jnp.exp(fade), spread) * lax.dot_general(
        read_ref[...],
        prior_ref[...].astype(jnp.bfloat16),
        across,
        preferred_element_type=jnp.float32,
    )
    place = lax.broadcasted_iota(jnp.int32, (1, columns), 1)
    for h in range(heads):
        differ = fade[:, h : h + 1] - fade_turned[h : h + 1, :]
        mixing = jnp.exp(jnp.where(causal, differ, very_low)) * match
        mine = (place >= h * channels) & (place < (h + 1) * channels)
        total += jnp.dot(
            mixing.astype(jnp.bfloat16),
            jnp.where(mine, scaled, 0.0).astype(jnp.bfloat16),
            preferred_element_type=jnp.float32,
        )
    gate = gate_ref[...].astype(jnp.float32)
    out_ref[...] = (total * (gate / (1.0 + jnp.exp(-gate)))).astype(jnp.bfloat16)


def scan_mixer(
    mixer_input, mixer_gate, state_in, state_out, step_size, decay_log, skip_gain, prior_state
):
    tokens, heads, channels = mixer_input.shape
    columns = heads * channels
    return pl.pallas_call(
        functools.partial(mixer_kernel, channels),
        out_shape=jax.ShapeDtypeStruct((tokens, columns), jnp.bfloat16),
        compiler_params=params(),
        name="mixer",
    )(
        mixer_input.reshape(tokens, columns),
        mixer_gate.reshape(tokens, columns),
        state_in,
        state_out,
        step_size,
        step_size.T,
        decay_log[None, :],
        decay_log[:, None],
        jnp.repeat(skip_gain, channels)[None, :],
        prior_state.reshape(columns, -1),
    )


def shifted(x, shift, axis):
    count = lax.axis_size(axis)
    return lax.ppermute(x, axis, [(i, (i + shift) % count) for i in range(count)])


def block_of(x, index, count, axis=0):
    rows = x.shape[axis] // count
    return lax.dynamic_slice_in_dim(x, index * rows, rows, axis)


def on_device(
    residual,
    queries,
    incoming_keys,
    incoming_values,
    cache_keys,
    cached_value_rows,
    context,
    attention_out,
    mixer_input,
    mixer_gate,
    state_in,
    state_out,
    step_size,
    decay_log,
    skip_gain,
    prior_state,
    mixer_out,
    norm_gain,
    hidden_gate,
    hidden_up,
    hidden_down,
):
    tokens, heads, depth = queries.shape
    shared_heads = cache_keys.shape[1]
    local_span = cache_keys.shape[0]
    fresh_count = incoming_keys.shape[0]
    owner_index = lax.axis_index(owners)
    owner_count = lax.axis_size("ctx") * lax.axis_size("row")
    head_index = lax.axis_index("head")
    head_count = lax.axis_size("head")

    gated = scan_mixer(
        mixer_input, mixer_gate, state_in, state_out, step_size, decay_log, skip_gain, prior_state
    )
    gated_all = lax.all_gather(gated, owners, axis=1, tiled=True)

    place = jnp.stack([context[0] - owner_index * local_span, owner_index * fresh_count])
    parts = attend(
        queries.reshape(tokens, -1),
        cache_keys.reshape(local_span, -1),
        cached_value_rows.reshape(local_span, -1),
        incoming_keys.reshape(fresh_count, -1),
        incoming_values.reshape(fresh_count, -1),
        place.astype(jnp.int32),
        heads,
        shared_heads,
    )
    swapped = lax.all_to_all(parts, owners, split_axis=0, concat_axis=0, tiled=True)
    attended = join(swapped.reshape(owner_count, fresh_count, -1), heads, depth)
    attended_all = lax.all_gather(attended, owners, axis=0, tiled=True)

    state_heads, channels = mixer_input.shape[1:]
    mixer_rows = (
        mixer_out.reshape(state_heads, owner_count, channels, -1)
        .transpose(1, 0, 2, 3)
        .reshape(mixer_out.shape)
    )
    mixer_part = jnp.dot(gated_all, mixer_rows, preferred_element_type=jnp.float32)
    branches = (
        jnp.dot(attended_all, attention_out, preferred_element_type=jnp.float32) + mixer_part
    )
    sent = branches.astype(jnp.bfloat16)
    for shift in range(1, head_count):
        branches += shifted(sent, shift, "head").astype(jnp.float32)
    combined = lax.all_to_all(
        branches.astype(jnp.bfloat16), owners, split_axis=0, concat_axis=1, tiled=True
    )
    trunk = (residual.astype(jnp.float32) + combined.astype(jnp.float32)).astype(jnp.bfloat16)
    trunk_wide = trunk.astype(jnp.float32)
    inverse_rms = lax.rsqrt(jnp.mean(trunk_wide * trunk_wide, axis=1, keepdims=True) + 1e-05)
    normed = (trunk_wide * inverse_rms * norm_gain[None, :]).astype(jnp.bfloat16)
    normed_part = block_of(normed, head_index, head_count, 1)
    segment = lax.all_gather(normed_part, owners, axis=0, tiled=True)

    units = hidden_gate.shape[1]
    pieces = 3 if units % (3 * lanes) == 0 else 1
    size = units // pieces
    share = tokens // head_count
    sums = []
    for c in range(pieces):
        columns = slice(c * size, (c + 1) * size)
        pair = jnp.concatenate(
            [
                jnp.dot(segment, hidden_gate[:, columns], preferred_element_type=jnp.float32),
                jnp.dot(segment, hidden_up[:, columns], preferred_element_type=jnp.float32),
            ],
            axis=1,
        )
        mine = block_of(pair, head_index, head_count)
        for shift in range(1, head_count):
            other = block_of(pair, (head_index + shift) % head_count, head_count)
            mine += shifted(other.astype(jnp.bfloat16), shift, "head").astype(jnp.float32)
        sums.append(mine)
    down = jnp.zeros((tokens, hidden_down.shape[1]), jnp.float32)
    for c in range(pieces):
        hidden_share = (jax.nn.silu(sums[c][:, :size]) * sums[c][:, size:]).astype(jnp.bfloat16)
        hidden = lax.dynamic_update_slice(
            jnp.zeros((tokens, size), jnp.bfloat16), hidden_share, (head_index * share, 0)
        )
        for shift in range(1, head_count):
            hidden = lax.dynamic_update_slice(
                hidden,
                shifted(hidden_share, shift, "head"),
                ((head_index - shift) % head_count * share, 0),
            )
        down += jnp.dot(
            hidden, hidden_down[c * size : (c + 1) * size], preferred_element_type=jnp.float32
        )
    down_rows = lax.psum_scatter(
        down.astype(jnp.bfloat16), owners, scatter_dimension=0, tiled=True
    )
    trunk_part = block_of(trunk_wide, head_index, head_count, 1)
    return (trunk_part + down_rows.astype(jnp.float32)).astype(jnp.bfloat16)


def solution(mesh):
    in_specs = (
        P(("groups", "ctx", "row"), None),
        P("groups", "head", None),
        P(("groups", "ctx", "row"), "head", None),
        P(("groups", "ctx", "row"), "head", None),
        P(("groups", "ctx", "row"), "head", None),
        P(("groups", "ctx", "row"), "head", None),
        P("groups"),
        P("head", ("ctx", "row")),
        P("groups", "head", ("ctx", "row")),
        P("groups", "head", ("ctx", "row")),
        P("groups", None),
        P("groups", None),
        P("groups", "head"),
        P("head"),
        P("head"),
        P(("groups", "head"), ("ctx", "row"), None),
        P("head", ("ctx", "row")),
        P(),
        P("head", ("ctx", "row")),
        P("head", ("ctx", "row")),
        P(("ctx", "row"), "head"),
    )
    out_specs = P(("groups", "ctx", "row"), "head")
    return jax.shard_map(
        on_device, mesh=mesh, in_specs=in_specs, out_specs=out_specs, check_vma=False
    )
```

```python
import functools
import math

import jax
import jax.numpy as jnp
from jax import lax
from jax.experimental import pallas as pl
from jax.experimental.pallas import tpu as pltpu
from jax.sharding import PartitionSpec as P

very_low = -1e30
least_peak = -1e29
owners = ("ctx", "row")
lanes = 128
vmem_limit = 48 * 1024 * 1024


def params():
    return pltpu.CompilerParams(vmem_limit_bytes=vmem_limit)


def in_thirds(x):
    first = x.astype(jnp.bfloat16)
    rest = x - first.astype(jnp.float32)
    second = rest.astype(jnp.bfloat16)
    third = (rest - second.astype(jnp.float32)).astype(jnp.bfloat16)
    return [t.astype(jnp.float32) for t in (first, second, third)]


def attend_kernel(
    heads, scale, place_ref, q_ref, k_ref, v_ref, fk_ref, fv_ref, out_ref, stats_ref
):
    head = pl.program_id(0)
    tokens, depth = q_ref.shape
    span, fresh = k_ref.shape[0], fk_ref.shape[0]
    across = (((1,), (1,)), ((), ()))
    query = q_ref[...]
    valid = place_ref[0]
    first_fresh = place_ref[1]
    scores = lax.dot_general(query, k_ref[...], across, preferred_element_type=jnp.float32) * scale
    position = lax.broadcasted_iota(jnp.int32, (1, span), 1)
    scores = jnp.where(position < valid, scores, very_low)
    new_scores = (
        lax.dot_general(query, fk_ref[...], across, preferred_element_type=jnp.float32) * scale
    )
    source = lax.broadcasted_iota(jnp.int32, (tokens, fresh), 1) + first_fresh
    target = lax.broadcasted_iota(jnp.int32, (tokens, fresh), 0)
    new_scores = jnp.where(source <= target, new_scores, very_low)
    peak = jnp.maximum(
        jnp.max(scores, axis=1, keepdims=True), jnp.max(new_scores, axis=1, keepdims=True)
    )
    peak = jnp.maximum(peak, least_peak)
    weights = jnp.exp(scores - peak)
    new_weights = jnp.exp(new_scores - peak)
    total = jnp.sum(weights, axis=1, keepdims=True) + jnp.sum(new_weights, axis=1, keepdims=True)
    mixed = jnp.dot(
        weights.astype(jnp.bfloat16), v_ref[...], preferred_element_type=jnp.float32
    ) + jnp.dot(new_weights.astype(jnp.bfloat16), fv_ref[...], preferred_element_type=jnp.float32)
    out_ref[:, pl.ds(pl.multiple_of(head * depth, depth), depth)] = (
        mixed / jnp.maximum(total, 1.0)
    ).astype(jnp.bfloat16)

    @pl.when(head == 0)
    def _():
        stats_ref[...] = jnp.zeros_like(stats_ref)

    lane = lax.broadcasted_iota(jnp.int32, stats_ref.shape, 1)
    held = stats_ref[...]
    for i, term in enumerate(in_thirds(peak) + in_thirds(total)):
        held = jnp.where(lane == head + i * heads, term, held)
    stats_ref[...] = held

    @pl.when(head == heads - 1)
    def _():
        out_ref[:, heads * depth :] = held.astype(jnp.bfloat16)


def attend(query_rows, keys, values, fresh_keys, fresh_values, place, heads, shared_heads):
    tokens = query_rows.shape[0]
    depth = query_rows.shape[1] // heads
    width = heads // shared_heads
    stat_lanes = -(-6 * heads // lanes) * lanes
    span, fresh = keys.shape[0], fresh_keys.shape[0]

    def of_group(rows):
        return pl.BlockSpec((rows, depth), lambda j: (0, j // width))

    out = (tokens, heads * depth + stat_lanes)
    return pl.pallas_call(
        functools.partial(attend_kernel, heads, 1.0 / math.sqrt(depth)),
        grid=(heads,),
        in_specs=[
            pl.BlockSpec(memory_space=pltpu.SMEM),
            pl.BlockSpec((tokens, depth), lambda j: (0, j)),
            of_group(span),
            of_group(span),
            of_group(fresh),
            of_group(fresh),
        ],
        out_specs=pl.BlockSpec(out, lambda j: (0, 0)),
        out_shape=jax.ShapeDtypeStruct(out, jnp.bfloat16),
        scratch_shapes=[pltpu.VMEM((tokens, stat_lanes), jnp.float32)],
        compiler_params=params(),
        name="attend",
        cost_estimate=pl.CostEstimate(
            flops=4 * tokens * heads * depth * span,
            bytes_accessed=4 * span * shared_heads * depth + 4 * tokens * heads * depth,
            transcendentals=tokens * heads * span,
        ),
    )(place, query_rows, keys, values, fresh_keys, fresh_values)


def join_kernel(heads, depth, in_ref, out_ref):
    stats = in_ref[:, :, heads * depth :].astype(jnp.float32)
    for j in range(heads):
        peak, total = (
            sum(stats[:, :, k * heads + j : k * heads + j + 1] for k in range(i, i + 3))
            for i in (0, 3)
        )
        share = total * jnp.exp(peak - jnp.max(peak, axis=0, keepdims=True))
        share = share / jnp.sum(share, axis=0, keepdims=True)
        piece = in_ref[:, :, j * depth : (j + 1) * depth].astype(jnp.float32)
        out_ref[:, j * depth : (j + 1) * depth] = jnp.sum(piece * share, axis=0).astype(
            jnp.bfloat16
        )


def join(parts, heads, depth):
    return pl.pallas_call(
        functools.partial(join_kernel, heads, depth),
        out_shape=jax.ShapeDtypeStruct((parts.shape[1], heads * depth), jnp.bfloat16),
        compiler_params=params(),
        name="join",
    )(parts)


def mixer_kernel(
    channels, x_ref, gate_ref, in_ref, read_ref, step_ref, turned_ref, decay_ref, decay_turned_ref,
    skip_ref, prior_ref, out_ref,
):
    tokens, columns = x_ref.shape
    heads = step_ref.shape[1]
    across = (((1,), (1,)), ((), ()))
    row = lax.broadcasted_iota(jnp.int32, (tokens, tokens), 0)
    col = lax.broadcasted_iota(jnp.int32, (tokens, tokens), 1)
    causal = row >= col
    exact = functools.partial(
        jnp.dot, precision=lax.Precision.HIGHEST, preferred_element_type=jnp.float32
    )
    step = step_ref[...]
    fade = exact(causal.astype(jnp.float32), step * -jnp.exp(decay_ref[...]))
    fade_turned = exact(
        turned_ref[...] * -jnp.exp(decay_turned_ref[...]), (row <= col).astype(jnp.float32)
    )
    owner = lax.broadcasted_iota(jnp.int32, (heads, columns), 0) * channels
    column = lax.broadcasted_iota(jnp.int32, (heads, columns), 1)
    spread = ((column >= owner) & (column < owner + channels)).astype(jnp.float32)
    x = x_ref[...].astype(jnp.float32)
    scaled = exact(step, spread) * x
    match = lax.dot_general(
        read_ref[...], in_ref[...], across, preferred_element_type=jnp.float32
    )
    total = skip_ref[...] * x + exact(jnp.exp(fade), spread) * lax.dot_general(
        read_ref[...],
        prior_ref[...].astype(jnp.bfloat16),
        across,
        preferred_element_type=jnp.float32,
    )
    place = lax.broadcasted_iota(jnp.int32, (1, columns), 1)
    for h in range(heads):
        differ = fade[:, h : h + 1] - fade_turned[h : h + 1, :]
        mixing = jnp.exp(jnp.where(causal, differ, very_low)) * match
        mine = (place >= h * channels) & (place < (h + 1) * channels)
        total += jnp.dot(
            mixing.astype(jnp.bfloat16),
            jnp.where(mine, scaled, 0.0).astype(jnp.bfloat16),
            preferred_element_type=jnp.float32,
        )
    gate = gate_ref[...].astype(jnp.float32)
    out_ref[...] = (total * (gate / (1.0 + jnp.exp(-gate)))).astype(jnp.bfloat16)


def scan_mixer(
    mixer_input, mixer_gate, state_in, state_out, step_size, decay_log, skip_gain, prior_state
):
    tokens, heads, channels = mixer_input.shape
    columns = heads * channels
    return pl.pallas_call(
        functools.partial(mixer_kernel, channels),
        out_shape=jax.ShapeDtypeStruct((tokens, columns), jnp.bfloat16),
        compiler_params=params(),
        name="mixer",
    )(
        mixer_input.reshape(tokens, columns),
        mixer_gate.reshape(tokens, columns),
        state_in,
        state_out,
        step_size,
        step_size.T,
        decay_log[None, :],
        decay_log[:, None],
        jnp.repeat(skip_gain, channels)[None, :],
        prior_state.reshape(columns, -1),
    )


def shifted(x, shift, axis):
    count = lax.axis_size(axis)
    return lax.ppermute(x, axis, [(i, (i + shift) % count) for i in range(count)])


def block_of(x, index, count, axis=0):
    rows = x.shape[axis] // count
    return lax.dynamic_slice_in_dim(x, index * rows, rows, axis)


def piece_cuts(units):
    tiles = units // lanes
    if units % lanes or tiles < 8:
        return [slice(0, units)]
    ends = [0] + [tiles * k // 21 * lanes for k in (3, 9, 15, 19)] + [units]
    return [slice(i, j) for i, j in zip(ends[:-1], ends[1:])]


def scatter_sums(x):
    ctx_count, row_count = lax.axis_size("ctx"), lax.axis_size("row")
    ctx_index, row_index = lax.axis_index("ctx"), lax.axis_index("row")
    blocks = x.reshape(ctx_count, row_count, -1, x.shape[1])

    def pick(array, index, axis):
        return lax.dynamic_index_in_dim(array, index, axis, False)

    mine = pick(blocks, row_index, 1)
    for shift in range(1, row_count):
        other = pick(blocks, (row_index + shift) % row_count, 1).astype(jnp.bfloat16)
        mine += shifted(other, shift, "row").astype(jnp.float32)
    total = pick(mine, ctx_index, 0)
    for shift in range(1, ctx_count):
        other = pick(mine, (ctx_index + shift) % ctx_count, 0).astype(jnp.bfloat16)
        total += shifted(other, shift, "ctx").astype(jnp.float32)
    return total


def on_device(
    residual,
    queries,
    incoming_keys,
    incoming_values,
    cache_keys,
    cached_value_rows,
    context,
    attention_out,
    mixer_input,
    mixer_gate,
    state_in,
    state_out,
    step_size,
    decay_log,
    skip_gain,
    prior_state,
    mixer_out,
    norm_gain,
    hidden_gate,
    hidden_up,
    hidden_down,
):
    tokens, heads, depth = queries.shape
    shared_heads = cache_keys.shape[1]
    local_span = cache_keys.shape[0]
    fresh_count = incoming_keys.shape[0]
    owner_index = lax.axis_index(owners)
    owner_count = lax.axis_size("ctx") * lax.axis_size("row")
    head_index = lax.axis_index("head")
    head_count = lax.axis_size("head")

    gated = scan_mixer(
        mixer_input, mixer_gate, state_in, state_out, step_size, decay_log, skip_gain, prior_state
    )
    gated_all = lax.all_gather(gated, owners, axis=1, tiled=True)

    place = jnp.stack([context[0] - owner_index * local_span, owner_index * fresh_count])
    parts = attend(
        queries.reshape(tokens, -1),
        cache_keys.reshape(local_span, -1),
        cached_value_rows.reshape(local_span, -1),
        incoming_keys.reshape(fresh_count, -1),
        incoming_values.reshape(fresh_count, -1),
        place.astype(jnp.int32),
        heads,
        shared_heads,
    )
    swapped = lax.all_to_all(parts, owners, split_axis=0, concat_axis=0, tiled=True)
    attended = join(swapped.reshape(owner_count, fresh_count, -1), heads, depth)
    attended_all = lax.all_gather(attended, owners, axis=0, tiled=True)

    state_heads, channels = mixer_input.shape[1:]
    mixer_rows = (
        mixer_out.reshape(state_heads, owner_count, channels, -1)
        .transpose(1, 0, 2, 3)
        .reshape(mixer_out.shape)
    )
    mixer_part = jnp.dot(gated_all, mixer_rows, preferred_element_type=jnp.float32)
    branches = (
        jnp.dot(attended_all, attention_out, preferred_element_type=jnp.float32) + mixer_part
    )
    sent = branches.astype(jnp.bfloat16)
    for shift in range(1, head_count):
        branches += shifted(sent, shift, "head").astype(jnp.float32)
    combined = lax.all_to_all(
        branches.astype(jnp.bfloat16), owners, split_axis=0, concat_axis=1, tiled=True
    )
    trunk = (residual.astype(jnp.float32) + combined.astype(jnp.float32)).astype(jnp.bfloat16)
    trunk_wide = trunk.astype(jnp.float32)
    inverse_rms = lax.rsqrt(jnp.mean(trunk_wide * trunk_wide, axis=1, keepdims=True) + 1e-05)
    normed = (trunk_wide * inverse_rms * norm_gain[None, :]).astype(jnp.bfloat16)
    normed_part = block_of(normed, head_index, head_count, 1)
    segment = lax.all_gather(normed_part, owners, axis=0, tiled=True)

    units = hidden_gate.shape[1]
    cuts = piece_cuts(units)
    share = tokens // head_count
    sums = []
    for columns in cuts:
        pair = jnp.concatenate(
            [
                jnp.dot(segment, hidden_gate[:, columns], preferred_element_type=jnp.float32),
                jnp.dot(segment, hidden_up[:, columns], preferred_element_type=jnp.float32),
            ],
            axis=1,
        )
        mine = block_of(pair, head_index, head_count)
        for shift in range(1, head_count):
            other = block_of(pair, (head_index + shift) % head_count, head_count)
            mine += shifted(other.astype(jnp.bfloat16), shift, "head").astype(jnp.float32)
        sums.append(mine)
    down = jnp.zeros((tokens, hidden_down.shape[1]), jnp.float32)
    for c, columns in enumerate(cuts):
        size = columns.stop - columns.start
        hidden_share = (jax.nn.silu(sums[c][:, :size]) * sums[c][:, size:]).astype(jnp.bfloat16)
        hidden = lax.dynamic_update_slice(
            jnp.zeros((tokens, size), jnp.bfloat16), hidden_share, (head_index * share, 0)
        )
        for shift in range(1, head_count):
            hidden = lax.dynamic_update_slice(
                hidden,
                shifted(hidden_share, shift, "head"),
                ((head_index - shift) % head_count * share, 0),
            )
        down += jnp.dot(
            hidden, hidden_down[columns], preferred_element_type=jnp.float32
        )
    halves = 2 if down.shape[1] % (2 * lanes) == 0 else 1
    down_rows = jnp.concatenate([scatter_sums(d) for d in jnp.split(down, halves, axis=1)], axis=1)
    trunk_part = block_of(trunk_wide, head_index, head_count, 1)
    return (trunk_part + down_rows).astype(jnp.bfloat16)


def solution(mesh):
    in_specs = (
        P(("groups", "ctx", "row"), None),
        P("groups", "head", None),
        P(("groups", "ctx", "row"), "head", None),
        P(("groups", "ctx", "row"), "head", None),
        P(("groups", "ctx", "row"), "head", None),
        P(("groups", "ctx", "row"), "head", None),
        P("groups"),
        P("head", ("ctx", "row")),
        P("groups", "head", ("ctx", "row")),
        P("groups", "head", ("ctx", "row")),
        P("groups", None),
        P("groups", None),
        P("groups", "head"),
        P("head"),
        P("head"),
        P(("groups", "head"), ("ctx", "row"), None),
        P("head", ("ctx", "row")),
        P(),
        P("head", ("ctx", "row")),
        P("head", ("ctx", "row")),
        P(("ctx", "row"), "head"),
    )
    out_specs = P(("groups", "ctx", "row"), "head")
    return jax.shard_map(
        on_device, mesh=mesh, in_specs=in_specs, out_specs=out_specs, check_vma=False
    )
```
